768 devices in a mesh: seq: 16 (over x_hi, y), rep: 48 (over x_lo, z, core).
Axes of the slice: x: 4 (x_hi: 2, x_lo: 2; x = x_hi * 2 + x_lo), y: 8, z: 12, core: 2. Of those that a mesh axis runs over, the one named last changes fastest.
Arguments:
- heads_out: bfloat16 [48, 2048, 4096], P('rep', None, 'seq'), may hold values from -6 to 6
- out_grad: bfloat16 [48, 2048, 2560], P('rep', 'seq'), may hold values from -0.125 to 0.125
- drop_mask: int32 [48], P('rep'), may hold values 0 or 1
- timestep: int32 [48], P('rep'), may hold values from 0 to 999
- error_old: bfloat16 [48, 4096, 2560], P('rep', 'seq'), may hold values from -4 to 4
- q_start: float32 [2560, 8], replicated, may hold values from -0.125 to 0.125
Outputs:
- q_new: float32 [2560, 8], replicated
- error_next: bfloat16 [48, 4096, 2560], P('rep', 'seq')
The draws below stay inside these ranges and needn't reach their ends.
All inputs are finite; a program needn't handle non-finite values. No bound on the sum of `drop_mask` on one device may be relied on, other than what follows from the above.
Results may differ from the reference program's by a relative error of at most 0.007.
Values may be sent and summed in bfloat16 or wider, within the bound.
No kernel may reach another device: no remote copies, remote signals or barrier semaphores. Data moves between devices by JAX's collectives and lax.ppermute only.
A program may use at most 64 MiB of HBM per device.

```python
import jax
import jax.numpy as jnp
from jax import lax

DOUT = 2560
RANK = 8
STEPS = 1000
HQ = 4096
SEQ_LEN = 2048
PROMPT = 128
N_REP = 48


def with_ends(entries, key, smallest, high):
    place = [jax.random.randint(jax.random.fold_in(key, axis), (), 0, length) for axis, length in enumerate(entries.shape)]
    main_axis = entries.shape.index(max(entries.shape))
    neighbour = place[:main_axis] + [(place[main_axis] + 1) % entries.shape[main_axis]] + place[main_axis + 1:]
    return entries.at[tuple(place)].set(smallest).at[tuple(neighbour)].set(high)


def block_levels(rng, dims, cuts, least, high):
    level, own = 1.0, jax.random.fold_in(rng, 6)
    for axis_at, blocks in cuts:
        steps = jnp.exp(jax.random.uniform(jax.random.fold_in(own, axis_at), (blocks,), jnp.float32, least / len(cuts), high / len(cuts)))
        level = level * jnp.repeat(steps, dims[axis_at] // blocks).reshape([-1 if axis == axis_at else 1 for axis in range(len(dims))])
    return level


def scatter_about(key, shape, deviation, reach, cuts=(), kind=jnp.bfloat16):
    drawn = jax.random.normal(key, shape, jnp.float32) * deviation
    if len(cuts) > 0:
        drawn = block_levels(key, shape, cuts, -0.22, 0.18) * drawn
    return jnp.clip(drawn, min=-reach, max=reach).astype(kind)


def setup_inputs(seed: int = 0) -> dict:
    seeds = jax.random.split(jax.random.key(seed), 7)
    return {
        "heads_out": scatter_about(seeds[0], (N_REP, SEQ_LEN, HQ), 1.0, 6.0, ((0, 48), (2, 16))),
        "out_grad": scatter_about(seeds[1], (N_REP, SEQ_LEN, DOUT), SEQ_LEN ** -0.5, 0.125, ((0, 48), (1, 16))),
        "drop_mask": with_ends((jax.random.randint(seeds[2], (N_REP,), 0, 2) < 1).astype(jnp.int32), jax.random.fold_in(seeds[2], 1), 0, 1),
        "timestep": with_ends(jax.random.randint(seeds[3], (N_REP,), 0, STEPS), jax.random.fold_in(seeds[3], 1), 0, STEPS - 1).astype(jnp.int32),
        "error_old": scatter_about(seeds[4], (N_REP, HQ, DOUT), 0.5, 4.0, ((0, 48), (1, 16))),
        "q_start": scatter_about(seeds[5], (DOUT, RANK), DOUT ** -0.5, 0.125, (), jnp.float32),
    }


highest = lax.Precision.HIGHEST

def token_weights(drop_mask, timestep):
    position = jnp.arange(SEQ_LEN)
    keeping = jnp.logical_or(position[None, :] >= PROMPT, drop_mask[:, None] == 1)
    scaling = 0.5 + 1.5 * timestep.astype(jnp.float32) / STEPS
    return jnp.where(keeping, 1.0, 0.0).astype(jnp.float32) * scaling[:, None]

def reference(heads_out, out_grad, drop_mask, timestep, error_old, q_start):
    weights = token_weights(drop_mask, timestep)
    weighted = (out_grad.astype(jnp.float32) * weights[:, :, None]).astype(jnp.bfloat16)

    def left_term(items):
        head_rows, grad_rows, error_rows = items
        projected = jnp.dot(grad_rows.astype(jnp.float32), q_start, precision=highest)
        first = jnp.dot(head_rows.astype(jnp.float32).T, projected, precision=highest)
        return first + jnp.dot(error_rows.astype(jnp.float32), q_start, precision=highest)
    left_total = jnp.sum(lax.map(left_term, (heads_out, weighted, error_old)), axis=0)
    gram = jnp.dot(left_total.T, left_total, precision=highest)
    lower = jnp.linalg.cholesky(gram)
    ortho_basis = jax.scipy.linalg.solve_triangular(lower, left_total.T, lower=True).T

    def right_term(items):
        head_rows, grad_rows, error_rows = items
        token_part = jnp.dot(head_rows.astype(jnp.float32), ortho_basis, precision=highest)
        first = jnp.dot(grad_rows.astype(jnp.float32).T, token_part, precision=highest)
        return first + jnp.dot(error_rows.astype(jnp.float32).T, ortho_basis, precision=highest)
    q_new = jnp.sum(lax.map(right_term, (heads_out, weighted, error_old)), axis=0) / N_REP
    decompressed = jnp.dot(ortho_basis, q_new.T, precision=highest)

    def new_error(items):
        head_rows, grad_rows, error_rows = items
        gradient = lax.dot_general(head_rows.astype(jnp.float32), grad_rows.astype(jnp.float32), (((0,), (0,)), ((), ())), preferred_element_type=jnp.float32)
        return (gradient + error_rows.astype(jnp.float32) - decompressed).astype(jnp.bfloat16)
    error_next = lax.map(new_error, (heads_out, weighted, error_old))
    return (q_new, error_next)
```

```python
import jax
import jax.numpy as jnp
from jax import lax
from jax.sharding import Mesh, PartitionSpec as P

STEPS = 1000
PROMPT = 128
SEQ = ("xh", "y")
REP = ("xl", "z", "c")
highest = lax.Precision.HIGHEST
f32 = jnp.float32
bf16 = jnp.bfloat16


def spread(x, axes):
    n = lax.axis_size(axes)
    return lax.all_to_all(jnp.broadcast_to(x[None], (n,) + x.shape), axes, 0, 0)


def body(heads_out, out_grad, drop_mask, timestep, error_old, q_start):
    tok = out_grad.shape[1]
    dout = out_grad.shape[2]
    rank = q_start.shape[1]
    half = lax.axis_index("xh")
    position = lax.axis_index(SEQ) * tok + jnp.arange(tok)
    keeping = jnp.logical_or(position >= PROMPT, drop_mask[0] == 1)
    scaling = 0.5 + 1.5 * timestep[0].astype(f32) / STEPS
    weights = jnp.where(keeping, 1.0, 0.0).astype(f32) * scaling
    weighted = (out_grad[0].astype(f32) * weights[:, None]).astype(bf16)
    heads = heads_out[0]
    error = error_old[0]
    n_tok, feats = heads.shape
    mine = n_tok // 2

    gathered = lax.all_gather(weighted, "y", axis=0, tiled=True)
    away = lax.dynamic_slice_in_dim(heads, (1 - half) * mine, mine, 0)
    here = lax.dynamic_slice_in_dim(heads, half * mine, mine, 0)
    swap = [(0, 1), (1, 0)]
    partner = lax.ppermute(away, "xh", swap)

    q_t = q_start.T
    proj = jnp.einsum("kd,td->kt", q_t, weighted.astype(f32), precision=highest)
    proj_all = spread(proj, SEQ)
    left_part = jnp.einsum("skt,stf->kf", proj_all, heads.astype(f32).reshape(16, tok, feats), precision=highest)
    left_part += jnp.einsum("kd,fd->kf", q_t, error.astype(f32), precision=highest)
    left = jnp.sum(spread(left_part, REP), axis=0)
    token_part = jnp.einsum("kf,stf->skt", left, heads.astype(f32).reshape(16, tok, feats), precision=highest)
    token = jnp.sum(lax.all_to_all(token_part, SEQ, 0, 0), axis=0)
    right_part = jnp.dot(token, weighted.astype(f32), precision=highest)
    right_part += jnp.dot(left, error.astype(f32), precision=highest)
    gram_part = jnp.dot(left, left.T, precision=highest)
    lanes = 128
    tiles = dout // lanes
    parts = right_part.reshape(rank, tiles, lanes).transpose(1, 0, 2)
    gram_tile = jnp.pad(gram_part, ((0, 0), (0, lanes - rank)))[None]
    parts = jnp.concatenate([parts, gram_tile, jnp.zeros((32 - tiles - 1, rank, lanes), f32)], axis=0)
    group = ("xh", "y", "c")
    tile = jnp.sum(lax.all_to_all(parts, group, 0, 0), axis=0)

    gathered, tile, partner = lax.optimization_barrier((gathered, tile, partner))
    dims = (((0,), (0,)), ((), ()))
    other_sum = lax.dot_general(partner, gathered, dims, preferred_element_type=f32).astype(bf16)
    from_partner = lax.ppermute(other_sum, "xh", swap)
    own_sum = lax.dot_general(here, gathered, dims, preferred_element_type=f32)

    tile = jnp.sum(spread(tile, ("xl", "z")), axis=0)
    whole = spread(tile, group)
    reps = lax.axis_size(REP)
    gram = whole[tiles][:, :rank] / reps
    right = whole[:tiles].transpose(1, 0, 2).reshape(rank, dout)
    work = jnp.concatenate([gram, jnp.eye(rank, dtype=f32)], axis=1)
    rows = jnp.arange(rank)
    for j in range(rank):
        pivot = work[j] * lax.rsqrt(work[j, j])
        below = jnp.where(rows > j, work[:, j] / jnp.sqrt(work[j, j]), 0.0)
        work = jnp.where((rows == j)[:, None], pivot[None], work - below[:, None] * pivot[None])
    inverse = work[:, rank:]
    basis = jnp.dot(inverse, left, precision=highest)
    q_new = jnp.dot(inverse, right, precision=highest) / reps
    decompressed = jnp.einsum("kf,kd->fd", basis, q_new, precision=highest)
    merged = own_sum + from_partner.astype(f32) + error.astype(f32)
    error_next = (merged - decompressed).astype(bf16)[None]
    return (q_new.T, error_next)


def solution(mesh):
    split = Mesh(mesh.devices.reshape(2, 8, 2, 12, 2), SEQ + REP)
    in_specs = (
        P(REP, None, SEQ),
        P(REP, SEQ, None),
        P(REP),
        P(REP),
        P(REP, SEQ, None),
        P(),
    )
    out_specs = (P(), P(REP, SEQ, None))
    return jax.shard_map(body, mesh=split, in_specs=in_specs, out_specs=out_specs, check_vma=False)
```

```python
import functools

import jax
import jax.numpy as jnp
from jax import lax
from jax.experimental import pallas as pl
from jax.experimental.pallas import tpu as pltpu
from jax.sharding import Mesh, PartitionSpec as P

STEPS = 1000
PROMPT = 128
SEQ = ("xh", "y")
REP = ("xl", "z", "c")
PAIR = ("xl", "z")
GROUP = ("xh", "y", "c")
LANES = 128
highest = lax.Precision.HIGHEST
f32 = jnp.float32
bf16 = jnp.bfloat16
VMEM = pl.BlockSpec(memory_space=pltpu.VMEM)
SMEM = pl.BlockSpec(memory_space=pltpu.SMEM)
NT = (((1,), (1,)), ((), ()))
TN = (((0,), (0,)), ((), ()))


def pieces(x):
    first = x.astype(bf16).astype(f32)
    rest = x - first
    second = rest.astype(bf16).astype(f32)
    return first, second, rest - second


def stacked(x):
    return jnp.concatenate(pieces(x) + (jnp.zeros_like(x),), axis=0).astype(bf16)


def folded(x):
    return x[0:8] + x[8:16] + x[16:24]


def call(kernel, outs, ins, flops, args):
    size = lambda a: a.size * a.dtype.itemsize
    moved = sum(size(a) for a in args) + sum(size(a) for a in outs)
    return pl.pallas_call(
        kernel,
        out_shape=outs,
        in_specs=ins,
        out_specs=[VMEM] * len(outs),
        cost_estimate=pl.CostEstimate(flops=flops, bytes_accessed=moved, transcendentals=0),
    )(*args)


def arr(shape, dtype):
    return jax.ShapeDtypeStruct(shape, dtype)


def weigh_kernel(drop_ref, step_ref, grad_ref, q_ref, weighted_ref, proj_ref):
    tok = grad_ref.shape[0]
    place = lax.axis_index("xh") * lax.axis_size("y") + lax.axis_index("y")
    position = place * tok + lax.broadcasted_iota(jnp.int32, (tok, 1), 0)
    drop = jnp.full((tok, 1), drop_ref[0], jnp.int32)
    step = jnp.full((tok, 1), step_ref[0], jnp.int32).astype(f32)
    keeping = jnp.logical_or(position >= PROMPT, drop == 1)
    weights = jnp.where(keeping, 0.5 + 1.5 * step / STEPS, 0.0)
    weighted = (grad_ref[...].astype(f32) * weights).astype(bf16)
    weighted_ref[...] = weighted
    proj = folded(lax.dot_general(stacked(q_ref[...]), weighted, NT, preferred_element_type=f32))
    for s in range(proj_ref.shape[0]):
        proj_ref[s] = proj


def error_left_kernel(q_ref, error_ref, out_ref):
    out_ref[...] = folded(lax.dot_general(stacked(q_ref[...]), error_ref[...], NT, preferred_element_type=f32))


def left_kernel(proj_ref, heads_ref, first_ref, out_ref):
    n, _, tok = proj_ref.shape
    proj = jnp.concatenate([proj_ref[s] for s in range(n)], axis=1)
    left = folded(jnp.dot(stacked(proj), heads_ref[...], preferred_element_type=f32)) + first_ref[...]
    for r in range(out_ref.shape[0]):
        out_ref[r] = left


def token_kernel(parts_ref, heads_ref, left_ref, out_ref):
    left = jnp.sum(parts_ref[...], axis=0)
    left_ref[...] = left
    token = folded(lax.dot_general(stacked(left), heads_ref[...], NT, preferred_element_type=f32))
    for s in range(out_ref.shape[0]):
        out_ref[s] = token[:, s * LANES:(s + 1) * LANES]


def error_right_kernel(left_ref, error_ref, right_ref, gram_ref):
    left = left_ref[...]
    right_ref[...] = folded(jnp.dot(stacked(left), error_ref[...], preferred_element_type=f32))
    rows = jnp.concatenate([left, jnp.zeros((LANES - 8, left.shape[1]), f32)], axis=0)
    gram_ref[...] = lax.dot_general(left, rows, NT, precision=highest, preferred_element_type=f32)


def right_kernel(token_ref, weighted_ref, right_ref, gram_ref, out_ref):
    token = jnp.sum(token_ref[...], axis=0)
    right = folded(jnp.dot(stacked(token), weighted_ref[...], preferred_element_type=f32)) + right_ref[...]
    tiles = right.shape[1] // LANES
    for t in range(tiles):
        out_ref[t] = right[:, t * LANES:(t + 1) * LANES]
    out_ref[tiles] = gram_ref[...]
    for t in range(tiles + 1, out_ref.shape[0]):
        out_ref[t] = jnp.zeros(out_ref.shape[1:], f32)


def sum_kernel(parts_ref, out_ref):
    total = jnp.sum(parts_ref[...], axis=0)
    for r in range(out_ref.shape[0]):
        out_ref[r] = total


def final_kernel(reps, gram_ref, whole_ref, left_ref, merged_ref, partner_ref, q_ref, out_ref, inverse, basis):
    @pl.when(pl.program_id(0) == 0)
    def _():
        rows = lax.broadcasted_iota(jnp.int32, (8, LANES), 0)
        lanes = lax.broadcasted_iota(jnp.int32, (8, LANES), 1)
        work = jnp.where(lanes < 8, gram_ref[0] / reps, jnp.where(lanes == rows + 8, 1.0, 0.0))
        for j in range(8):
            root = jnp.sqrt(work[j:j + 1, j:j + 1])
            pivot = work[j:j + 1, :] / root
            below = work[:, j:j + 1] / root
            work = jnp.where(rows == j, pivot, jnp.where(rows > j, work - below * pivot, work))
        inverse[...] = work
        left = left_ref[...]
        total = jnp.zeros_like(left)
        for k in range(8):
            total += work[:, 8 + k:9 + k] * left[k:k + 1, :]
        one, two, three = pieces(total)
        zero = jnp.zeros_like(total)
        basis[...] = jnp.concatenate([one, one, one, two, two, three, zero, zero], axis=0).astype(bf16)

    work = inverse[...]
    right = jnp.concatenate([whole_ref[t] for t in range(whole_ref.shape[0])], axis=1)
    q_new = jnp.zeros_like(right)
    for k in range(8):
        q_new += work[:, 8 + k:9 + k] * right[k:k + 1, :]
    q_new = q_new / reps
    q_ref[...] = q_new
    one, two, three = pieces(q_new)
    zero = jnp.zeros_like(q_new)
    factor = jnp.concatenate([one, two, three, one, two, one, zero, zero], axis=0).astype(bf16)
    taken = lax.dot_general(basis[...], factor, TN, preferred_element_type=f32)
    out_ref[...] = (merged_ref[...] + partner_ref[...].astype(f32) - taken).astype(bf16)


def exchange(x, axes):
    return lax.all_to_all(x, axes, 0, 0)


def body(heads_out, out_grad, drop_mask, timestep, error_old, q_start):
    weighed, heads, error = out_grad[0], heads_out[0], error_old[0]
    tok, dout = weighed.shape
    n_tok, feats = heads.shape
    rank = q_start.shape[1]
    mine = n_tok // 2
    tiles = dout // LANES
    half = lax.axis_index("xh")
    n_seq, n_rep = lax.axis_size(SEQ), lax.axis_size(REP)
    n_pair, n_group = lax.axis_size(PAIR), lax.axis_size(GROUP)
    q_t = q_start.T

    weighted, proj = call(
        weigh_kernel,
        [arr((tok, dout), bf16), arr((n_seq, rank, tok), f32)],
        [SMEM, SMEM, VMEM, VMEM],
        2 * 32 * tok * dout,
        (drop_mask, timestep, weighed, q_t),
    )
    gathered = lax.all_gather(weighted, "y", axis=0, tiled=True)
    away = lax.dynamic_slice_in_dim(heads, (1 - half) * mine, mine, 0)
    here = lax.dynamic_slice_in_dim(heads, half * mine, mine, 0)
    swap = [(0, 1), (1, 0)]
    partner = lax.ppermute(away, "xh", swap)

    (first,) = call(error_left_kernel, [arr((rank, feats), f32)], [VMEM] * 2, 2 * 32 * feats * dout, (q_t, error))
    (parts,) = call(
        left_kernel,
        [arr((n_rep, rank, feats), f32)],
        [VMEM] * 3,
        2 * 32 * n_tok * feats,
        (exchange(proj, SEQ), heads, first),
    )
    left, token = call(
        token_kernel,
        [arr((rank, feats), f32), arr((n_seq, rank, tok), f32)],
        [VMEM] * 2,
        2 * 32 * n_tok * feats,
        (exchange(parts, REP), heads),
    )
    right, gram = call(
        error_right_kernel,
        [arr((rank, dout), f32), arr((rank, LANES), f32)],
        [VMEM] * 2,
        2 * 32 * feats * dout,
        (left, error),
    )
    (pieces_out,) = call(
        right_kernel,
        [arr((n_group, rank, LANES), f32)],
        [VMEM] * 4,
        2 * 32 * tok * dout,
        (exchange(token, SEQ), weighted, right, gram),
    )
    (tile,) = call(sum_kernel, [arr((n_pair, rank, LANES), f32)], [VMEM], n_group * rank * LANES, (exchange(pieces_out, GROUP),))

    gathered, tile, partner = lax.optimization_barrier((gathered, tile, partner))
    other_sum = lax.dot_general(partner, gathered, TN, preferred_element_type=f32).astype(bf16)
    (tile,) = call(sum_kernel, [arr((n_group, rank, LANES), f32)], [VMEM], n_pair * rank * LANES, (exchange(tile, PAIR),))
    tile, other_sum, gathered, here = lax.optimization_barrier((tile, other_sum, gathered, here))
    from_partner = lax.ppermute(other_sum, "xh", swap)
    merged = lax.dot_general(here, gathered, TN, preferred_element_type=f32) + error.astype(f32)
    whole = exchange(tile, GROUP)

    wide = 4
    cols = wide * LANES
    q_new, error_next = pl.pallas_call(
        functools.partial(final_kernel, float(n_rep)),
        grid=(tiles // wide,),
        out_shape=[arr((rank, dout), f32), arr((feats, dout), bf16)],
        in_specs=[
            pl.BlockSpec((1, rank, LANES), lambda i: (tiles, 0, 0)),
            pl.BlockSpec((wide, rank, LANES), lambda i: (i, 0, 0)),
            pl.BlockSpec((rank, feats), lambda i: (0, 0)),
            pl.BlockSpec((feats, cols), lambda i: (0, i)),
            pl.BlockSpec((feats, cols), lambda i: (0, i)),
        ],
        out_specs=[
            pl.BlockSpec((rank, cols), lambda i: (0, i)),
            pl.BlockSpec((feats, cols), lambda i: (0, i)),
        ],
        scratch_shapes=[pltpu.VMEM((8, LANES), f32), pltpu.VMEM((64, feats), bf16)],
        cost_estimate=pl.CostEstimate(flops=2 * 64 * feats * dout, bytes_accessed=8 * feats * dout, transcendentals=0),
    )(whole, whole, left, merged, from_partner)
    return (q_new.T, error_next[None])


def solution(mesh):
    split = Mesh(mesh.devices.reshape(2, 8, 2, 12, 2), SEQ + REP)
    in_specs = (
        P(REP, None, SEQ),
        P(REP, SEQ, None),
        P(REP),
        P(REP),
        P(REP, SEQ, None),
        P(),
    )
    out_specs = (P(), P(REP, SEQ, None))
    return jax.shard_map(body, mesh=split, in_specs=in_specs, out_specs=out_specs, check_vma=False)
```

```python
import functools

import jax
import jax.numpy as jnp
from jax import lax
from jax.experimental import pallas as pl
from jax.experimental.pallas import tpu as pltpu
from jax.sharding import Mesh, PartitionSpec as P

STEPS = 1000
PROMPT = 128
SEQ = ("xh", "y")
REP = ("xl", "z", "c")
PAIR = ("z", "c")
GROUP = ("xh", "y", "xl")
LANES = 128
highest = lax.Precision.HIGHEST
f32 = jnp.float32
bf16 = jnp.bfloat16
VMEM = pl.BlockSpec(memory_space=pltpu.VMEM)
SMEM = pl.BlockSpec(memory_space=pltpu.SMEM)
NT = (((1,), (1,)), ((), ()))
TN = (((0,), (0,)), ((), ()))


def pieces(x):
    first = x.astype(bf16).astype(f32)
    rest = x - first
    second = rest.astype(bf16).astype(f32)
    return first, second, rest - second


def stacked(x):
    return jnp.concatenate(pieces(x) + (jnp.zeros_like(x),), axis=0).astype(bf16)


def folded(x):
    return x[0:8] + x[8:16] + x[16:24]


def call(kernel, outs, ins, flops, args, limit=0):
    size = lambda a: a.size * a.dtype.itemsize
    moved = sum(size(a) for a in args) + sum(size(a) for a in outs)
    return pl.pallas_call(
        kernel,
        out_shape=outs,
        in_specs=ins,
        out_specs=[VMEM] * len(outs),
        compiler_params=pltpu.CompilerParams(vmem_limit_bytes=limit) if limit else None,
        cost_estimate=pl.CostEstimate(flops=flops, bytes_accessed=moved, transcendentals=0),
    )(*args)


def arr(shape, dtype):
    return jax.ShapeDtypeStruct(shape, dtype)


def weigh_kernel(drop_ref, step_ref, grad_ref, q_ref, weighted_ref, proj_ref):
    tok = grad_ref.shape[0]
    place = lax.axis_index("xh") * lax.axis_size("y") + lax.axis_index("y")
    position = place * tok + lax.broadcasted_iota(jnp.int32, (tok, 1), 0)
    drop = jnp.full((tok, 1), drop_ref[0], jnp.int32)
    step = jnp.full((tok, 1), step_ref[0], jnp.int32).astype(f32)
    keeping = jnp.logical_or(position >= PROMPT, drop == 1)
    weights = jnp.where(keeping, 0.5 + 1.5 * step / STEPS, 0.0)
    weighted = (grad_ref[...].astype(f32) * weights).astype(bf16)
    weighted_ref[...] = weighted
    proj = folded(lax.dot_general(stacked(q_ref[...]), weighted, NT, preferred_element_type=f32))
    for s in range(proj_ref.shape[0]):
        proj_ref[s] = proj


def factor_kernel(reps, whole_ref, left_ref, q_ref, basis_ref, factor_ref):
    tiles = q_ref.shape[1] // LANES
    rows = lax.broadcasted_iota(jnp.int32, (8, LANES), 0)
    lanes = lax.broadcasted_iota(jnp.int32, (8, LANES), 1)
    work = jnp.where(lanes < 8, whole_ref[tiles] / reps, jnp.where(lanes == rows + 8, 1.0, 0.0))
    for j in range(8):
        column = jnp.broadcast_to(work[:, j:j + 1], (8, LANES))
        scale = 1.0 / jnp.sqrt(column[j:j + 1, :])
        pivot = work[j:j + 1, :] * scale
        work = jnp.where(rows == j, pivot, jnp.where(rows > j, work - column * scale * pivot, work))

    left = left_ref[...]
    right = jnp.concatenate([whole_ref[t] for t in range(tiles)], axis=1)
    basis = jnp.zeros_like(left)
    q_new = jnp.zeros_like(right)
    for k in range(8):
        weight = work[:, 8 + k:9 + k]
        basis += weight * left[k:k + 1, :]
        q_new += weight * right[k:k + 1, :]
    q_new = q_new / reps
    q_ref[...] = q_new
    one, two, three = pieces(basis)
    zero = jnp.zeros_like(basis)
    basis_ref[...] = jnp.concatenate([one, one, one, two, two, three, zero, zero], axis=0).astype(bf16)
    one, two, three = pieces(q_new)
    zero = jnp.zeros_like(q_new)
    factor_ref[...] = jnp.concatenate([one, two, three, one, two, one, zero, zero], axis=0).astype(bf16)


def exchange(x, axes):
    return lax.all_to_all(x, axes, 0, 0)


def spread(x, axes):
    return exchange(jnp.broadcast_to(x[None], (lax.axis_size(axes),) + x.shape), axes)


def body(heads_out, out_grad, drop_mask, timestep, error_old, q_start):
    heads, error = heads_out[0], error_old[0]
    tok, dout = out_grad.shape[1:]
    n_tok, feats = heads.shape
    rank = q_start.shape[1]
    tiles = dout // LANES
    half = lax.axis_index("xh")
    n_seq, n_rep, n_group = lax.axis_size(SEQ), lax.axis_size(REP), lax.axis_size(GROUP)
    q_t = q_start.T
    wide_heads = heads.astype(f32).reshape(n_seq, tok, feats)

    weighted, proj = call(
        weigh_kernel,
        [arr((tok, dout), bf16), arr((n_seq, rank, tok), f32)],
        [SMEM, SMEM, VMEM, VMEM],
        2 * 32 * tok * dout,
        (drop_mask, timestep, out_grad[0], q_t),
    )
    swap = [(0, 1), (1, 0)]
    gathered = lax.all_gather(weighted, "y", axis=0, tiled=True)
    mine = n_tok // lax.axis_size("xh")
    partner = lax.ppermute(lax.dynamic_slice_in_dim(heads, (1 - half) * mine, mine, 0), "xh", swap)
    here = lax.dynamic_slice_in_dim(heads, half * mine, mine, 0)

    first = jnp.einsum("kd,fd->kf", q_t, error.astype(f32), precision=highest)
    proj, first = lax.optimization_barrier((exchange(proj, SEQ), first))
    left_part = jnp.einsum("skt,stf->kf", proj, wide_heads, precision=highest) + first
    left = jnp.sum(spread(left_part, REP), axis=0)
    token_part = jnp.einsum("kf,stf->skt", left, wide_heads, precision=highest)
    right_error = jnp.dot(left, error.astype(f32), precision=highest)
    gram_part = jnp.dot(left, left.T, precision=highest)
    token, right_error, gram_part = lax.optimization_barrier((exchange(token_part, SEQ), right_error, gram_part))
    token = jnp.sum(token, axis=0)
    right_part = jnp.dot(token, weighted.astype(f32), precision=highest) + right_error
    parts = right_part.reshape(rank, tiles, LANES).transpose(1, 0, 2)
    gram_tile = jnp.pad(gram_part, ((0, 0), (0, LANES - rank)))[None]
    parts = jnp.concatenate([parts, gram_tile, jnp.zeros((n_group - tiles - 1, rank, LANES), f32)], axis=0)
    other_sum = lax.dot_general(partner, gathered, TN, preferred_element_type=f32).astype(bf16)
    parts, other_sum = lax.optimization_barrier((exchange(parts, GROUP), other_sum))
    tile = jnp.sum(parts, axis=0)
    from_partner = lax.ppermute(other_sum, "xh", swap)
    tile = jnp.sum(spread(tile, PAIR), axis=0)
    own_sum = lax.dot_general(here, gathered, TN, preferred_element_type=f32) + error.astype(f32)
    whole, own_sum = lax.optimization_barrier((spread(tile, GROUP), own_sum))
    q_new, basis, factor = call(
        functools.partial(factor_kernel, float(n_rep)),
        [arr((rank, dout), f32), arr((8 * rank, feats), bf16), arr((8 * rank, dout), bf16)],
        [VMEM] * 2,
        100 * rank * dout,
        (whole, left),
        8 << 20,
    )
    taken = lax.dot_general(basis, factor, TN, preferred_element_type=f32)
    error_next = (own_sum + from_partner.astype(f32) - taken).astype(bf16)
    return (q_new.T, error_next[None])


def solution(mesh):
    split = Mesh(mesh.devices.reshape(2, 8, 2, 12, 2), SEQ + REP)
    in_specs = (
        P(REP, None, SEQ),
        P(REP, SEQ, None),
        P(REP),
        P(REP),
        P(REP, SEQ, None),
        P(),
    )
    out_specs = (P(), P(REP, SEQ, None))
    return jax.shard_map(body, mesh=split, in_specs=in_specs, out_specs=out_specs, check_vma=False)
```

```python
import functools

import jax
import jax.numpy as jnp
from jax import lax
from jax.experimental import pallas as pl
from jax.experimental.pallas import tpu as pltpu
from jax.sharding import Mesh, PartitionSpec as P

STEPS = 1000
PROMPT = 128
SEQ = ("xh", "y")
REP = ("xl", "z", "c")
PAIR = ("z", "c")
GROUP = ("xh", "y", "xl")
LANES = 128
highest = lax.Precision.HIGHEST
f32 = jnp.float32
bf16 = jnp.bfloat16
VMEM = pl.BlockSpec(memory_space=pltpu.VMEM)
SMEM = pl.BlockSpec(memory_space=pltpu.SMEM)
NT = (((1,), (1,)), ((), ()))
TN = (((0,), (0,)), ((), ()))


def pieces(x):
    first = x.astype(bf16).astype(f32)
    rest = x - first
    second = rest.astype(bf16).astype(f32)
    return first, second, rest - second


def stacked(x):
    return jnp.concatenate(pieces(x) + (jnp.zeros_like(x),), axis=0).astype(bf16)


def folded(x):
    return x[0:8] + x[8:16] + x[16:24]


def call(kernel, outs, ins, flops, args, limit=0):
    size = lambda a: a.size * a.dtype.itemsize
    moved = sum(size(a) for a in args) + sum(size(a) for a in outs)
    return pl.pallas_call(
        kernel,
        out_shape=outs,
        in_specs=ins,
        out_specs=[VMEM] * len(outs),
        compiler_params=pltpu.CompilerParams(vmem_limit_bytes=limit) if limit else None,
        cost_estimate=pl.CostEstimate(flops=flops, bytes_accessed=moved, transcendentals=0),
    )(*args)


def arr(shape, dtype):
    return jax.ShapeDtypeStruct(shape, dtype)


def weigh_kernel(drop_ref, step_ref, grad_ref, q_ref, weighted_ref, keep_ref, send_ref, proj_ref):
    tok = grad_ref.shape[0]
    place = lax.axis_index("xh") * lax.axis_size("y") + lax.axis_index("y")
    position = place * tok + lax.broadcasted_iota(jnp.int32, (tok, 1), 0)
    drop = jnp.full((tok, 1), drop_ref[0], jnp.int32)
    step = jnp.full((tok, 1), step_ref[0], jnp.int32).astype(f32)
    keeping = jnp.logical_or(position >= PROMPT, drop == 1)
    weights = jnp.where(keeping, 0.5 + 1.5 * step / STEPS, 0.0)
    weighted = (grad_ref[...].astype(f32) * weights).astype(bf16)
    weighted_ref[...] = weighted
    cut = keep_ref.shape[1]
    low, high = weighted[:, :cut], weighted[:, cut:]

    @pl.when(lax.axis_index("xh") == 0)
    def _():
        keep_ref[...] = low
        send_ref[...] = high

    @pl.when(lax.axis_index("xh") == 1)
    def _():
        keep_ref[...] = high
        send_ref[...] = low

    proj = folded(lax.dot_general(stacked(q_ref[...]), weighted, NT, preferred_element_type=f32))
    for s in range(proj_ref.shape[0]):
        proj_ref[s] = proj


def factor_kernel(reps, whole_ref, left_ref, q_ref, basis_ref, factor_ref):
    tiles = q_ref.shape[1] // LANES
    rows = lax.broadcasted_iota(jnp.int32, (8, LANES), 0)
    lanes = lax.broadcasted_iota(jnp.int32, (8, LANES), 1)
    work = jnp.where(lanes < 8, whole_ref[tiles] / reps, jnp.where(lanes == rows + 8, 1.0, 0.0))
    for j in range(8):
        column = jnp.broadcast_to(work[:, j:j + 1], (8, LANES))
        scale = 1.0 / jnp.sqrt(column[j:j + 1, :])
        pivot = work[j:j + 1, :] * scale
        work = jnp.where(rows == j, pivot, jnp.where(rows > j, work - column * scale * pivot, work))

    left = left_ref[...]
    right = jnp.concatenate([whole_ref[t] for t in range(tiles)], axis=1)
    basis = jnp.zeros_like(left)
    q_new = jnp.zeros_like(right)
    for k in range(8):
        weight = work[:, 8 + k:9 + k]
        basis += weight * left[k:k + 1, :]
        q_new += weight * right[k:k + 1, :]
    q_new = q_new / reps
    q_ref[...] = q_new
    one, two, three = pieces(basis)
    zero = jnp.zeros_like(basis)
    basis_ref[...] = jnp.concatenate([one, one, one, two, two, three, zero, zero], axis=0).astype(bf16)
    one, two, three = pieces(q_new)
    zero = jnp.zeros_like(q_new)
    factor_ref[...] = jnp.concatenate([one, two, three, one, two, one, zero, zero], axis=0).astype(bf16)


def exchange(x, axes):
    return lax.all_to_all(x, axes, 0, 0)


def spread(x, axes):
    return exchange(jnp.broadcast_to(x[None], (lax.axis_size(axes),) + x.shape), axes)


def body(heads_out, out_grad, drop_mask, timestep, error_old, q_start):
    heads, error = heads_out[0], error_old[0]
    tok, dout = out_grad.shape[1:]
    n_tok, feats = heads.shape
    rank = q_start.shape[1]
    tiles = dout // LANES
    half = lax.axis_index("xh")
    n_seq, n_rep, n_group = lax.axis_size(SEQ), lax.axis_size(REP), lax.axis_size(GROUP)
    q_t = q_start.T
    wide_heads = heads.astype(f32).reshape(n_seq, tok, feats)

    weighted, keep, send, proj = call(
        weigh_kernel,
        [arr((tok, dout), bf16), arr((tok, dout // 2), bf16), arr((tok, dout // 2), bf16), arr((n_seq, rank, tok), f32)],
        [SMEM, SMEM, VMEM, VMEM],
        2 * 32 * tok * dout,
        (drop_mask, timestep, out_grad[0], q_t),
    )
    swap = [(0, 1), (1, 0)]
    received = lax.ppermute(send, "xh", swap)
    low = half == 0
    rows = jnp.concatenate([jnp.where(low, keep, received), jnp.where(low, received, keep)], axis=0)
    first = jnp.einsum("kd,fd->kf", q_t, error.astype(f32), precision=highest)
    proj, rows, first = lax.optimization_barrier((exchange(proj, SEQ), rows, first))
    gathered = lax.all_gather(rows, "y", axis=0, tiled=True)
    halves = lax.axis_size("xh")
    own = heads.reshape(halves, n_seq // halves, tok, feats).transpose(1, 0, 2, 3).reshape(n_tok, feats)
    own = lax.optimization_barrier(own)
    early, late = jnp.split(own, 2)
    early = lax.ppermute(early, "xh", swap)

    left_part = jnp.einsum("skt,stf->kf", proj, wide_heads, precision=highest) + first
    cores = lax.axis_size("c")
    share = feats // cores
    left_part = lax.psum(left_part, "c")
    left_part = lax.dynamic_slice_in_dim(left_part, lax.axis_index("c") * share, share, 1)
    left = jnp.sum(spread(left_part, REP).reshape(n_rep // cores, cores, rank, share), axis=0)
    left = jnp.concatenate([left[i] for i in range(cores)], axis=1)
    late, _ = lax.optimization_barrier((late, left))
    late = lax.ppermute(late, "xh", swap)
    partner = jnp.concatenate([early, late], axis=0)
    token_part = jnp.einsum("kf,stf->skt", left, wide_heads, precision=highest)
    right_error = jnp.dot(left, error.astype(f32), precision=highest)
    gram_part = jnp.dot(left, left.T, precision=highest)
    token, right_error, gram_part = lax.optimization_barrier((exchange(token_part, SEQ), right_error, gram_part))
    token = jnp.sum(token, axis=0)
    right_part = jnp.dot(token, weighted.astype(f32), precision=highest) + right_error
    parts = right_part.reshape(rank, tiles, LANES).transpose(1, 0, 2)
    gram_tile = jnp.pad(gram_part, ((0, 0), (0, LANES - rank)))[None]
    parts = jnp.concatenate([parts, gram_tile, jnp.zeros((n_group - tiles - 1, rank, LANES), f32)], axis=0)
    tile = jnp.sum(exchange(parts, GROUP), axis=0)
    other_sum = lax.dot_general(partner, gathered, TN, preferred_element_type=f32).astype(bf16)
    from_partner = lax.ppermute(other_sum, "xh", swap)
    parts, _ = lax.optimization_barrier((spread(tile, PAIR), other_sum))
    tile = jnp.sum(parts, axis=0)
    own_sum = lax.dot_general(own, gathered, TN, preferred_element_type=f32)
    whole, own_sum = lax.optimization_barrier((spread(tile, GROUP), own_sum))
    q_new, basis, factor = call(
        functools.partial(factor_kernel, float(n_rep)),
        [arr((rank, dout), f32), arr((8 * rank, feats), bf16), arr((8 * rank, dout), bf16)],
        [VMEM] * 2,
        100 * rank * dout,
        (whole, left),
        8 << 20,
    )
    taken = lax.dot_general(basis, factor, TN, preferred_element_type=f32)
    cut = dout // 2
    far = from_partner.astype(f32)
    sums = [jnp.where(low, own_sum, far), jnp.where(low, far, own_sum)]
    error_next = [
        (sums[i] + error[:, i * cut:(i + 1) * cut].astype(f32) - taken[:, i * cut:(i + 1) * cut]).astype(bf16)
        for i in range(2)
    ]
    error_next = jnp.concatenate(error_next, axis=1)
    return (q_new.T, error_next[None])


def solution(mesh):
    split = Mesh(mesh.devices.reshape(2, 8, 2, 12, 2), SEQ + REP)
    in_specs = (
        P(REP, None, SEQ),
        P(REP, SEQ, None),
        P(REP),
        P(REP),
        P(REP, SEQ, None),
        P(),
    )
    out_specs = (P(), P(REP, SEQ, None))
    return jax.shard_map(body, mesh=split, in_specs=in_specs, out_specs=out_specs, check_vma=False)
```

```python
import functools

import jax
import jax.numpy as jnp
from jax import lax
from jax.experimental import pallas as pl
from jax.experimental.pallas import tpu as pltpu
from jax.sharding import Mesh, PartitionSpec as P

STEPS = 1000
PROMPT = 128
SEQ = ("xh", "y")
REP = ("xl", "z", "c")
PAIR = ("z", "c")
GROUP = ("xh", "y", "xl")
LANES = 128
highest = lax.Precision.HIGHEST
f32 = jnp.float32
bf16 = jnp.bfloat16
VMEM = pl.BlockSpec(memory_space=pltpu.VMEM)
SMEM = pl.BlockSpec(memory_space=pltpu.SMEM)
NT = (((1,), (1,)), ((), ()))
TN = (((0,), (0,)), ((), ()))


def pieces(x):
    first = x.astype(bf16).astype(f32)
    rest = x - first
    second = rest.astype(bf16).astype(f32)
    return first, second, rest - second


def stacked(x):
    return jnp.concatenate(pieces(x) + (jnp.zeros_like(x),), axis=0).astype(bf16)


def folded(x):
    return x[0:8] + x[8:16] + x[16:24]


def call(kernel, outs, ins, flops, args, limit=0):
    size = lambda a: a.size * a.dtype.itemsize
    moved = sum(size(a) for a in args) + sum(size(a) for a in outs)
    return pl.pallas_call(
        kernel,
        out_shape=outs,
        in_specs=ins,
        out_specs=[VMEM] * len(outs),
        compiler_params=pltpu.CompilerParams(vmem_limit_bytes=limit) if limit else None,
        cost_estimate=pl.CostEstimate(flops=flops, bytes_accessed=moved, transcendentals=0),
    )(*args)


def arr(shape, dtype):
    return jax.ShapeDtypeStruct(shape, dtype)


def weigh_kernel(drop_ref, step_ref, grad_ref, q_ref, weighted_ref, keep_ref, send_ref, proj_ref, split_ref):
    tok = grad_ref.shape[0]
    place = lax.axis_index("xh") * lax.axis_size("y") + lax.axis_index("y")
    position = place * tok + lax.broadcasted_iota(jnp.int32, (tok, 1), 0)
    drop = jnp.full((tok, 1), drop_ref[0], jnp.int32)
    step = jnp.full((tok, 1), step_ref[0], jnp.int32).astype(f32)
    keeping = jnp.logical_or(position >= PROMPT, drop == 1)
    weights = jnp.where(keeping, 0.5 + 1.5 * step / STEPS, 0.0)
    weighted = (grad_ref[...].astype(f32) * weights).astype(bf16)
    weighted_ref[...] = weighted
    cut = keep_ref.shape[1]
    low, high = weighted[:, :cut], weighted[:, cut:]

    @pl.when(lax.axis_index("xh") == 0)
    def _():
        keep_ref[...] = low
        send_ref[...] = high

    @pl.when(lax.axis_index("xh") == 1)
    def _():
        keep_ref[...] = high
        send_ref[...] = low

    split_ref[...] = stacked(q_ref[...])
    proj = folded(lax.dot_general(split_ref[...], weighted, NT, preferred_element_type=f32))
    for s in range(proj_ref.shape[0]):
        proj_ref[s] = proj


def factor_kernel(reps, whole_ref, left_ref, q_ref, basis_ref, factor_ref):
    tiles = q_ref.shape[1] // LANES
    rows = lax.broadcasted_iota(jnp.int32, (8, LANES), 0)
    lanes = lax.broadcasted_iota(jnp.int32, (8, LANES), 1)
    work = jnp.where(lanes < 8, whole_ref[tiles] / reps, jnp.where(lanes == rows + 8, 1.0, 0.0))
    for j in range(8):
        column = jnp.broadcast_to(work[:, j:j + 1], (8, LANES))
        scale = 1.0 / jnp.sqrt(column[j:j + 1, :])
        pivot = work[j:j + 1, :] * scale
        work = jnp.where(rows == j, pivot, jnp.where(rows > j, work - column * scale * pivot, work))

    left = left_ref[...]
    right = jnp.concatenate([whole_ref[t] for t in range(tiles)], axis=1)
    basis = jnp.zeros_like(left)
    q_new = jnp.zeros_like(right)
    for k in range(8):
        weight = work[:, 8 + k:9 + k]
        basis += weight * left[k:k + 1, :]
        q_new += weight * right[k:k + 1, :]
    q_new = q_new / reps
    q_ref[...] = q_new
    one, two, three = pieces(basis)
    zero = jnp.zeros_like(basis)
    basis_ref[...] = jnp.concatenate([one, one, one, two, two, three, zero, zero], axis=0).astype(bf16)
    one, two, three = pieces(q_new)
    zero = jnp.zeros_like(q_new)
    factor_ref[...] = jnp.concatenate([one, two, three, one, two, one, zero, zero], axis=0).astype(bf16)


def exchange(x, axes):
    return lax.all_to_all(x, axes, 0, 0)


def spread(x, axes):
    return exchange(jnp.broadcast_to(x[None], (lax.axis_size(axes),) + x.shape), axes)


def body(heads_out, out_grad, drop_mask, timestep, error_old, q_start):
    heads, error = heads_out[0], error_old[0]
    tok, dout = out_grad.shape[1:]
    n_tok, feats = heads.shape
    rank = q_start.shape[1]
    tiles = dout // LANES
    half = lax.axis_index("xh")
    n_seq, n_rep, n_group = lax.axis_size(SEQ), lax.axis_size(REP), lax.axis_size(GROUP)
    q_t = q_start.T
    wide_heads = heads.astype(f32).reshape(n_seq, tok, feats)

    weighted, keep, send, proj, q_split = call(
        weigh_kernel,
        [arr((tok, dout), bf16), arr((tok, dout // 2), bf16), arr((tok, dout // 2), bf16), arr((n_seq, rank, tok), f32), arr((4 * rank, dout), bf16)],
        [SMEM, SMEM, VMEM, VMEM],
        2 * 32 * tok * dout,
        (drop_mask, timestep, out_grad[0], q_t),
    )
    swap = [(0, 1), (1, 0)]
    received = lax.ppermute(send, "xh", swap)
    low = half == 0
    rows = jnp.concatenate([jnp.where(low, keep, received), jnp.where(low, received, keep)], axis=0)
    first = folded(lax.dot_general(q_split, error, NT, preferred_element_type=f32))
    proj, rows, first = lax.optimization_barrier((exchange(proj, SEQ), rows, first))
    gathered = lax.all_gather(rows, "y", axis=0, tiled=True)
    halves = lax.axis_size("xh")
    own = heads.reshape(halves, n_seq // halves, tok, feats).transpose(1, 0, 2, 3).reshape(n_tok, feats)
    own = lax.optimization_barrier(own)
    early, late = jnp.split(own, 2)
    early = lax.ppermute(early, "xh", swap)

    left_part = jnp.einsum("skt,stf->kf", proj, wide_heads, precision=highest) + first
    cores = lax.axis_size("c")
    share = feats // cores
    left_part = lax.psum(left_part, "c")
    left_part = lax.dynamic_slice_in_dim(left_part, lax.axis_index("c") * share, share, 1)
    left = jnp.sum(spread(left_part, REP).reshape(n_rep // cores, cores, rank, share), axis=0)
    left = jnp.concatenate([left[i] for i in range(cores)], axis=1)
    late, _ = lax.optimization_barrier((late, left))
    late = lax.ppermute(late, "xh", swap)
    partner = jnp.concatenate([early, late], axis=0)
    token_part = jnp.einsum("kf,stf->skt", left, wide_heads, precision=highest)
    right_error = jnp.dot(left, error.astype(f32), precision=highest)
    gram_part = jnp.dot(left, left.T, precision=highest)
    token, right_error, gram_part = lax.optimization_barrier((exchange(token_part, SEQ), right_error, gram_part))
    token = jnp.sum(token, axis=0)
    right_part = jnp.dot(token, weighted.astype(f32), precision=highest) + right_error
    parts = right_part.reshape(rank, tiles, LANES).transpose(1, 0, 2)
    gram_tile = jnp.pad(gram_part, ((0, 0), (0, LANES - rank)))[None]
    parts = jnp.concatenate([parts, gram_tile, jnp.zeros((n_group - tiles - 1, rank, LANES), f32)], axis=0)
    tile = jnp.sum(exchange(parts, GROUP), axis=0)
    other_sum = lax.dot_general(partner, gathered, TN, preferred_element_type=f32).astype(bf16)
    from_partner = lax.ppermute(other_sum, "xh", swap)
    parts, _ = lax.optimization_barrier((spread(tile, PAIR), other_sum))
    tile = jnp.sum(parts, axis=0)
    own_sum = lax.dot_general(own, gathered, TN, preferred_element_type=f32)
    whole, own_sum = lax.optimization_barrier((spread(tile, GROUP), own_sum))
    q_new, basis, factor = call(
        functools.partial(factor_kernel, float(n_rep)),
        [arr((rank, dout), f32), arr((8 * rank, feats), bf16), arr((8 * rank, dout), bf16)],
        [VMEM] * 2,
        100 * rank * dout,
        (whole, left),
        8 << 20,
    )
    taken = lax.dot_general(basis, factor, TN, preferred_element_type=f32)
    cut = dout // 2
    far = from_partner.astype(f32)
    sums = [jnp.where(low, own_sum, far), jnp.where(low, far, own_sum)]
    error_next = [
        (sums[i] + error[:, i * cut:(i + 1) * cut].astype(f32) - taken[:, i * cut:(i + 1) * cut]).astype(bf16)
        for i in range(2)
    ]
    error_next = jnp.concatenate(error_next, axis=1)
    return (q_new.T, error_next[None])


def solution(mesh):
    split = Mesh(mesh.devices.reshape(2, 8, 2, 12, 2), SEQ + REP)
    in_specs = (
        P(REP, None, SEQ),
        P(REP, SEQ, None),
        P(REP),
        P(REP),
        P(REP, SEQ, None),
        P(),
    )
    out_specs = (P(), P(REP, SEQ, None))
    return jax.shard_map(body, mesh=split, in_specs=in_specs, out_specs=out_specs, check_vma=False)
```
